256 devices in a mesh: island: 32 (over z_hi, x, y), fsdp: 8 (over z_lo, core).
Axes of the slice: x: 4, y: 4, z: 8 (z_hi: 2, z_lo: 4; z = z_hi * 4 + z_lo), core: 2. Of those that a mesh axis runs over, the one named last changes fastest.
Arguments:
- global_weights: float32 [256, 28672], P('fsdp'), may hold values from -4 to 4
- local_weights: float32 [32, 256, 28672], P('island', 'fsdp')
- momentum: float32 [256, 28672], P('fsdp', 'island'), may hold values from -0.6 to 0.6
Outputs:
- new_global: float32 [256, 28672], P('fsdp')
- new_momentum: float32 [256, 28672], P('fsdp', 'island')
The draws below stay inside these ranges and needn't reach their ends.
All inputs are finite; a program needn't handle non-finite values.
Results may differ from the reference program's by a relative error of at most 0.00002.
Values sent between devices are 32-bit elements; how exact they have to be, the bound alone decides.
No kernel may reach another device: no remote copies, remote signals or barrier semaphores. Data moves between devices by JAX's collectives and lax.ppermute only.
A program may use at most 64 MiB of HBM per device.

```python
import math
import jax
import jax.numpy as jnp
from jax import lax

FF = 28672
ROWS = 256
N_ISLAND = 32


def shared_global(key):
    return jnp.clip(jax.random.normal(key, (ROWS, FF), jnp.float32), -4.0, 4.0)


def draw_global_weights(key, part):
    return shared_global(key)


def draw_local_weights(key, part):
    base = shared_global(key)
    key = jax.random.fold_in(key, 7)
    keys = jax.random.split(key, 3)
    rows_pos = jnp.arange(ROWS, dtype=jnp.float32) / ROWS
    cols_pos = jnp.arange(FF, dtype=jnp.float32) / FF
    row_scale = 10.0 ** rows_pos * jnp.exp(jax.random.uniform(keys[0], (ROWS,), jnp.float32, -math.log(2.0), math.log(2.0)))
    col_scale = 10.0 ** cols_pos * jnp.exp(jax.random.uniform(keys[1], (FF,), jnp.float32, -math.log(2.0), math.log(2.0)))
    noise = jnp.clip(jax.random.normal(keys[2], (N_ISLAND, ROWS, FF), jnp.float32), -6.0, 6.0)
    return base[None] - 0.1 * noise * row_scale[None, :, None] * col_scale[None, None, :]


def levels(key, dims, cuts, least, top_value):
    def one(dim, shards_of):
        steps = jax.random.uniform(jax.random.fold_in(jax.random.fold_in(key, 6), dim), (shards_of,), jnp.float32, least / len(cuts), top_value / len(cuts))
        return jnp.repeat(jnp.exp(steps), dims[dim] // shards_of).reshape((-1,) + (1,) * (len(dims) - dim - 1))

    gain = one(*cuts[0])
    for cut in cuts[1:]:
        gain = gain * one(*cut)
    return gain


def bell_draw(key, shape, width, bound, cuts=(), held_as=jnp.bfloat16):
    level = levels(key, shape, cuts, -0.22, 0.18) if cuts else 1.0
    drawn = jax.random.normal(key, shape, jnp.float32) * width * level
    return jnp.minimum(jnp.maximum(drawn, -bound), bound).astype(held_as)


def setup_inputs(seed: int = 0) -> dict:
    streams_of = jax.random.split(jax.random.key(seed), 4)
    global_weights = draw_global_weights(jax.random.fold_in(streams_of[3], 71), 0)
    local_weights = draw_local_weights(jax.random.fold_in(streams_of[3], 71), 0)
    momentum = bell_draw(streams_of[2], (ROWS, FF), 0.1, 0.6, ((0, 8), (1, 32)), jnp.float32)
    return {"global_weights": global_weights, "local_weights": local_weights, "momentum": momentum}


clip_level = 0.1
outer_rate = 0.7
moment_decay = 0.9

def reference(global_weights, local_weights, momentum):

    def add_island(total, local):
        return (total + (global_weights - local), None)
    total, unused = lax.scan(add_island, jnp.zeros_like(global_weights), local_weights)
    average = total / N_ISLAND
    spread = jnp.sqrt(jnp.mean(average * average) + 1e-06)
    factor = jnp.minimum(1.0, clip_level / spread)
    clipped = factor * average
    new_momentum = moment_decay * momentum + clipped
    new_global = global_weights - outer_rate * (clipped + moment_decay * new_momentum)
    return (new_global, new_momentum)
```

```python
import functools

import jax
import jax.numpy as jnp
from jax import lax
from jax.experimental import pallas as pl
from jax.experimental.pallas import tpu as pltpu
from jax.sharding import PartitionSpec as P

clip_level = 0.1
outer_rate = 0.7
moment_decay = 0.9

AXES = ("island", "fsdp")
HALVES, SIDE, RUN, CORES = 2, 4, 4, 2


def pairs(move):
    out = []
    for zh in range(HALVES):
        for x in range(SIDE):
            for y in range(SIDE):
                for zl in range(RUN):
                    for core in range(CORES):
                        there = move(zh, x, y, zl, core)
                        place = lambda h, i, j, k, c: ((h * SIDE + i) * SIDE + j) * RUN * CORES + k * CORES + c
                        out.append((place(zh, x, y, zl, core), place(*there)))
    return out


def along(first, step):
    def move(zh, x, y, zl, core):
        if (core == 0) == first:
            return zh, (x + step) % SIDE, y, zl, core
        return zh, x, (y + step) % SIDE, zl, core

    return pairs(move)


FIRST = {step: along(True, step) for step in (1, 2, 3)}
SECOND = {step: along(False, step) for step in (1, 2, 3)}
ACROSS = pairs(lambda zh, x, y, zl, core: (1 - zh, x, y, zl, core))
UP = {step: pairs(lambda zh, x, y, zl, core, s=step: (zh, x, y, (zl + s) % RUN, core)) for step in (1, 2, 3)}
TWIN = pairs(lambda zh, x, y, zl, core: (zh, x, y, zl, 1 - core))


def send(value, route):
    return lax.ppermute(value, AXES, route)


def place_of(width, step, near, half):
    island = lax.axis_index("island")
    core = lax.rem(lax.axis_index("fsdp"), CORES)
    zh = island // (SIDE * SIDE)
    x = lax.rem(island // SIDE, SIDE)
    y = lax.rem(island, SIDE)
    one = jnp.where(core == 0, x, y)
    two = jnp.where(core == 0, y, x)
    one = lax.rem(one + step, SIDE)
    two = lax.rem(two + near, SIDE)
    zh = lax.rem(zh + half, HALVES)
    block = zh * SIDE * SIDE + jnp.where(core == 0, one * SIDE + two, two * SIDE + one)
    return pl.multiple_of(block * width, 128)


def pack_kernel(step, width, whole, piece, sems):
    copies = []
    for near in range(SIDE):
        for half in range(HALVES):
            n = near * HALVES + half
            copy = pltpu.make_async_copy(
                whole.at[:, pl.ds(place_of(width, step, near, half), width)], piece.at[near, half], sems.at[n]
            )
            copy.start()
            copies.append(copy)
    for copy in copies:
        copy.wait()


def pack(whole, step, width):
    rows = whole.shape[0]
    return pl.pallas_call(
        functools.partial(pack_kernel, step, width),
        out_shape=jax.ShapeDtypeStruct((SIDE, HALVES, rows, width), whole.dtype),
        in_specs=[pl.BlockSpec(memory_space=pl.ANY)],
        out_specs=pl.BlockSpec(memory_space=pl.ANY),
        scratch_shapes=[pltpu.SemaphoreType.DMA((SIDE * HALVES,))],
        cost_estimate=pl.CostEstimate(flops=0, bytes_accessed=2 * 4 * SIDE * HALVES * rows * width, transcendentals=0),
        name=f"pack{step}",
    )(whole)


def unpack_kernel(step, width, piece, *rest):
    whole, sems = rest[-2], rest[-1]
    copies = []
    for near in range(SIDE):
        for half in range(HALVES):
            n = near * HALVES + half
            copy = pltpu.make_async_copy(
                piece.at[near, half], whole.at[:, pl.ds(place_of(width, step, near, half), width)], sems.at[n]
            )
            copy.start()
            copies.append(copy)
    for copy in copies:
        copy.wait()


def unpack(piece, whole, step, shape):
    _, _, rows, width = piece.shape
    given = [] if whole is None else [whole]
    return pl.pallas_call(
        functools.partial(unpack_kernel, step, width),
        out_shape=jax.ShapeDtypeStruct(shape, piece.dtype),
        in_specs=[pl.BlockSpec(memory_space=pl.ANY)] * (1 + len(given)),
        out_specs=pl.BlockSpec(memory_space=pl.ANY),
        scratch_shapes=[pltpu.SemaphoreType.DMA((SIDE * HALVES,))],
        input_output_aliases={1: 0} if given else {},
        cost_estimate=pl.CostEstimate(flops=0, bytes_accessed=2 * 4 * SIDE * HALVES * rows * width, transcendentals=0),
        name=f"unpack{step}",
    )(piece, *given)


def per_device(global_weights, local_weights, momentum):
    islands = lax.axis_size("island")
    shards = lax.axis_size("fsdp")
    rows, columns = global_weights.shape
    width = columns // islands
    local = local_weights[0]

    arrived = [send(pack(local, step, width), FIRST[step]) for step in (2, 1, 3)]
    base = pack(global_weights, 0, width)
    mine = pack(local, 0, width)
    parts = []
    for near in range(SIDE):
        total = base[near] - mine[near]
        for piece in arrived:
            total = total + (base[near] - piece[near])
        parts.append(total)
    got = [send(parts[step], SECOND[step]) for step in (2, 1, 3)]
    half = parts[0] + got[0] + got[1] + got[2]
    summed = half[0] + send(half[1], ACROSS)
    average = summed / islands

    count = rows * columns * shards
    squares = jnp.sum(average * average).reshape(1, 1)
    squares = jnp.broadcast_to(squares, (8, 128))
    squares = squares + send(squares, TWIN)
    for route in (FIRST, SECOND, UP):
        squares = squares + send(squares, route[1]) + send(squares, route[2]) + send(squares, route[3])
    squares = squares + send(squares, ACROSS)
    spread = jnp.sqrt(squares[0, 0] / count + 1e-06)
    factor = jnp.minimum(1.0, clip_level / spread)

    clipped = factor * average
    new_momentum = moment_decay * momentum + clipped
    updated = base[0, 0] - outer_rate * (clipped + moment_decay * new_momentum)

    both = jnp.stack([updated, send(updated, ACROSS)])
    near = [None] * SIDE
    near[0] = both
    for step in (2, 1, 3):
        near[SIDE - step] = send(both, SECOND[step])
    piece = jnp.stack(near)
    new_global = None
    others = [(SIDE - step, send(piece, FIRST[step])) for step in (2, 1, 3)]
    for place, got in [(0, piece)] + others:
        new_global = unpack(got, new_global, place, (rows, columns))
    return (new_global, new_momentum)


def solution(mesh):
    placed = (P("fsdp", None), P("island", "fsdp", None), P("fsdp", "island"))
    return jax.shard_map(
        per_device,
        mesh=mesh,
        in_specs=placed,
        out_specs=(P("fsdp", None), P("fsdp", "island")),
        check_vma=False,
    )
```

```python
import functools

import jax
import jax.numpy as jnp
from jax import lax
from jax.experimental import pallas as pl
from jax.experimental.pallas import tpu as pltpu
from jax.sharding import PartitionSpec as P

clip_level = 0.1
outer_rate = 0.7
moment_decay = 0.9

AXES = ("island", "fsdp")
HALVES, SIDE, RUN, CORES = 2, 4, 4, 2


def pairs(move):
    out = []
    for zh in range(HALVES):
        for x in range(SIDE):
            for y in range(SIDE):
                for zl in range(RUN):
                    for core in range(CORES):
                        there = move(zh, x, y, zl, core)
                        place = lambda h, i, j, k, c: ((h * SIDE + i) * SIDE + j) * RUN * CORES + k * CORES + c
                        out.append((place(zh, x, y, zl, core), place(*there)))
    return out


def along(first, step):
    def move(zh, x, y, zl, core):
        if (core == 0) == first:
            return zh, (x + step) % SIDE, y, zl, core
        return zh, x, (y + step) % SIDE, zl, core

    return pairs(move)


FIRST = {step: along(True, step) for step in (1, 2, 3)}
SECOND = {step: along(False, step) for step in (1, 2, 3)}
ACROSS = pairs(lambda zh, x, y, zl, core: (1 - zh, x, y, zl, core))
UP = {step: pairs(lambda zh, x, y, zl, core, s=step: (zh, x, y, (zl + s) % RUN, core)) for step in (1, 2, 3)}
TWIN = pairs(lambda zh, x, y, zl, core: (zh, x, y, zl, 1 - core))


def send(value, route):
    return lax.ppermute(value, AXES, route)


def place_of(width, step, near, half):
    island = lax.axis_index("island")
    core = lax.rem(lax.axis_index("fsdp"), CORES)
    zh = island // (SIDE * SIDE)
    x = lax.rem(island // SIDE, SIDE)
    y = lax.rem(island, SIDE)
    one = jnp.where(core == 0, x, y)
    two = jnp.where(core == 0, y, x)
    one = lax.rem(one + step, SIDE)
    two = lax.rem(two + near, SIDE)
    zh = lax.rem(zh + half, HALVES)
    block = zh * SIDE * SIDE + jnp.where(core == 0, one * SIDE + two, two * SIDE + one)
    return pl.multiple_of(block * width, 128)


def pack_kernel(step, width, whole, piece, sems):
    copies = []
    for near in range(SIDE):
        for half in range(HALVES):
            n = near * HALVES + half
            copy = pltpu.make_async_copy(
                whole.at[:, pl.ds(place_of(width, step, near, half), width)], piece.at[near, half], sems.at[n]
            )
            copy.start()
            copies.append(copy)
    for copy in copies:
        copy.wait()


def pack(whole, step, width):
    rows = whole.shape[0]
    return pl.pallas_call(
        functools.partial(pack_kernel, step, width),
        out_shape=jax.ShapeDtypeStruct((SIDE, HALVES, rows, width), whole.dtype),
        in_specs=[pl.BlockSpec(memory_space=pltpu.HBM)],
        out_specs=pl.BlockSpec(memory_space=pltpu.VMEM),
        scratch_shapes=[pltpu.SemaphoreType.DMA((SIDE * HALVES,))],
        cost_estimate=pl.CostEstimate(flops=0, bytes_accessed=2 * 4 * SIDE * HALVES * rows * width, transcendentals=0),
        name=f"pack{step}",
    )(whole)


def unpack_kernel(step, width, piece, *rest):
    whole, sems = rest[-2], rest[-1]
    copies = []
    for near in range(SIDE):
        for half in range(HALVES):
            n = near * HALVES + half
            copy = pltpu.make_async_copy(
                piece.at[near, half], whole.at[:, pl.ds(place_of(width, step, near, half), width)], sems.at[n]
            )
            copy.start()
            copies.append(copy)
    for copy in copies:
        copy.wait()


def unpack(piece, whole, step, shape):
    _, _, rows, width = piece.shape
    given = [] if whole is None else [whole]
    return pl.pallas_call(
        functools.partial(unpack_kernel, step, width),
        out_shape=jax.ShapeDtypeStruct(shape, piece.dtype),
        in_specs=[pl.BlockSpec(memory_space=pltpu.VMEM)] + [pl.BlockSpec(memory_space=pltpu.HBM)] * len(given),
        out_specs=pl.BlockSpec(memory_space=pltpu.HBM),
        scratch_shapes=[pltpu.SemaphoreType.DMA((SIDE * HALVES,))],
        input_output_aliases={1: 0} if given else {},
        cost_estimate=pl.CostEstimate(flops=0, bytes_accessed=2 * 4 * SIDE * HALVES * rows * width, transcendentals=0),
        name=f"unpack{step}",
    )(piece, *given)


def per_device(global_weights, local_weights, momentum):
    islands = lax.axis_size("island")
    shards = lax.axis_size("fsdp")
    rows, columns = global_weights.shape
    width = columns // islands
    local = local_weights[0]

    arrived = [send(pack(local, step, width), FIRST[step]) for step in (2, 1, 3)]
    base = pack(global_weights, 0, width)
    mine = pack(local, 0, width)
    parts = []
    for near in range(SIDE):
        total = base[near] - mine[near]
        for piece in arrived:
            total = total + (base[near] - piece[near])
        parts.append(total)
    got = [send(parts[step], SECOND[step]) for step in (2, 1, 3)]
    half = parts[0] + got[0] + got[1] + got[2]
    summed = half[0] + send(half[1], ACROSS)
    average = summed / islands

    count = rows * columns * shards
    squares = jnp.sum(average * average).reshape(1, 1)
    squares = jnp.broadcast_to(squares, (8, 128))
    squares = squares + send(squares, TWIN)
    for route in (FIRST, SECOND, UP):
        squares = squares + send(squares, route[1]) + send(squares, route[2]) + send(squares, route[3])
    squares = squares + send(squares, ACROSS)
    spread = jnp.sqrt(squares[0, 0] / count + 1e-06)
    factor = jnp.minimum(1.0, clip_level / spread)

    clipped = factor * average
    new_momentum = moment_decay * momentum + clipped
    updated = base[0, 0] - outer_rate * (clipped + moment_decay * new_momentum)

    both = jnp.stack([updated, send(updated, ACROSS)])
    near = [None] * SIDE
    near[0] = both
    for step in (2, 1, 3):
        near[SIDE - step] = send(both, SECOND[step])
    piece = jnp.stack(near)
    new_global = None
    others = [(SIDE - step, send(piece, FIRST[step])) for step in (2, 1, 3)]
    for place, got in [(0, piece)] + others:
        new_global = unpack(got, new_global, place, (rows, columns))
    return (new_global, new_momentum)


def solution(mesh):
    placed = (P("fsdp", None), P("island", "fsdp", None), P("fsdp", "island"))
    return jax.shard_map(
        per_device,
        mesh=mesh,
        in_specs=placed,
        out_specs=(P("fsdp", None), P("fsdp", "island")),
        check_vma=False,
    )
```

```python
import functools

import jax
import jax.numpy as jnp
from jax import lax
from jax.experimental import pallas as pl
from jax.experimental.pallas import tpu as pltpu
from jax.sharding import PartitionSpec as P

clip_level = 0.1
outer_rate = 0.7
moment_decay = 0.9

AXES = ("island", "fsdp")
HALVES, SIDE, RUN, CORES = 2, 4, 4, 2
BLOCKS = 2 * HALVES
ROOM = 16 * 2**20


def pairs(move):
    out = []
    for zh in range(HALVES):
        for x in range(SIDE):
            for y in range(SIDE):
                for zl in range(RUN):
                    for core in range(CORES):
                        there = move(zh, x, y, zl, core)
                        place = lambda h, i, j, k, c: ((h * SIDE + i) * SIDE + j) * RUN * CORES + k * CORES + c
                        out.append((place(zh, x, y, zl, core), place(*there)))
    return out


def along(first, step):
    def move(zh, x, y, zl, core):
        if (core == 0) == first:
            return zh, (x + step) % SIDE, y, zl, core
        return zh, x, (y + step) % SIDE, zl, core

    return pairs(move)


FIRST = {step: along(True, step) for step in (1, 2, 3)}
SECOND = {step: along(False, step) for step in (1, 2, 3)}
ACROSS = pairs(lambda zh, x, y, zl, core: (1 - zh, x, y, zl, core))
UP = {step: pairs(lambda zh, x, y, zl, core, s=step: (zh, x, y, (zl + s) % RUN, core)) for step in (1, 2, 3)}
TWIN = pairs(lambda zh, x, y, zl, core: (zh, x, y, zl, 1 - core))


def send(value, route):
    return lax.ppermute(value, AXES, route)


def place_of(width, step, near, half):
    island = lax.axis_index("island")
    core = lax.rem(lax.axis_index("fsdp"), CORES)
    zh = island // (SIDE * SIDE)
    x = lax.rem(island // SIDE, SIDE)
    y = lax.rem(island, SIDE)
    one = jnp.where(core == 0, x, y)
    two = jnp.where(core == 0, y, x)
    one = lax.rem(one + step, SIDE)
    two = lax.rem(two + near, SIDE)
    zh = lax.rem(zh + half, HALVES)
    block = zh * SIDE * SIDE + jnp.where(core == 0, one * SIDE + two, two * SIDE + one)
    return pl.multiple_of(block * width, 128)


def blocks_of(groups):
    return [(step, 2 * group + k, half) for step, group in groups for k in range(2) for half in range(HALVES)]


def pack_kernel(jobs, width, *refs):
    sems = refs[-1]
    inputs = len(refs) - 1 - len(jobs)
    copies = []
    for n, (source, step) in enumerate(jobs):
        for near in range(SIDE):
            for half in range(HALVES):
                copy = pltpu.make_async_copy(
                    refs[source].at[:, pl.ds(place_of(width, step, near, half), width)],
                    refs[inputs + n].at[near, half],
                    sems.at[len(copies)],
                )
                copy.start()
                copies.append(copy)
    for copy in copies:
        copy.wait()


def pack(sources, jobs, width, behind=()):
    rows = sources[0].shape[0]
    amount = len(jobs) * SIDE * HALVES
    return pl.pallas_call(
        functools.partial(pack_kernel, jobs, width),
        out_shape=[jax.ShapeDtypeStruct((SIDE, HALVES, rows, width), sources[0].dtype)] * len(jobs),
        in_specs=[pl.BlockSpec(memory_space=pltpu.HBM)] * len(sources)
        + [pl.BlockSpec(memory_space=pl.ANY)] * len(behind),
        out_specs=[pl.BlockSpec(memory_space=pltpu.VMEM)] * len(jobs),
        scratch_shapes=[pltpu.SemaphoreType.DMA((amount,))],
        cost_estimate=pl.CostEstimate(flops=0, bytes_accessed=8 * amount * rows * width, transcendentals=0),
        compiler_params=pltpu.CompilerParams(vmem_limit_bytes=ROOM),
        name=f"pack{len(jobs)}",
    )(*sources, *behind)


def unpack_kernel(groups, width, *refs):
    pieces, (whole, sems) = refs[: len(groups)], refs[-2:]
    copies = []
    for n, block in enumerate(blocks_of(groups)):
        group, k, half = n // BLOCKS, (n % BLOCKS) // HALVES, n % HALVES
        copy = pltpu.make_async_copy(
            pieces[group].at[k, half], whole.at[:, pl.ds(place_of(width, *block), width)], sems.at[n]
        )
        copy.start()
        copies.append(copy)
    for copy in copies:
        copy.wait()


def unpack(groups, pieces, whole, shape):
    rows, width = pieces[0].shape[-2:]
    given = [] if whole is None else [whole]
    vmem, hbm = pl.BlockSpec(memory_space=pltpu.VMEM), pl.BlockSpec(memory_space=pltpu.HBM)
    amount = len(groups) * BLOCKS
    return pl.pallas_call(
        functools.partial(unpack_kernel, groups, width),
        out_shape=jax.ShapeDtypeStruct(shape, pieces[0].dtype),
        in_specs=[vmem] * len(groups) + [hbm] * len(given),
        out_specs=hbm,
        scratch_shapes=[pltpu.SemaphoreType.DMA((amount,))],
        input_output_aliases={len(groups): 0} if given else {},
        cost_estimate=pl.CostEstimate(flops=0, bytes_accessed=8 * amount * rows * width, transcendentals=0),
        compiler_params=pltpu.CompilerParams(vmem_limit_bytes=ROOM),
        name=f"unpack{len(groups)}",
    )(*pieces, *given)


def spread_near(value):
    near = [value] + [None] * (SIDE - 1)
    for step in (2, 1, 3):
        near[SIDE - step] = send(value, SECOND[step])
    return near


def after(value, *others):
    return lax.optimization_barrier((value,) + others)[0]


def per_device(global_weights, local_weights, momentum):
    islands = lax.axis_size("island")
    shards = lax.axis_size("fsdp")
    rows, columns = global_weights.shape
    width = columns // islands
    local = local_weights[0]

    (far,) = pack((local,), ((0, 2),), width)
    right, left = pack((local,), ((0, 1), (0, 3)), width, (far,))
    far = send(far, FIRST[2])
    packed = left
    right, left = send(right, FIRST[1]), send(left, FIRST[3])
    base, mine = pack((global_weights, local), ((0, 0), (1, 0)), width, (packed,))
    speed = after(momentum, base)
    speed = jnp.stack([speed, send(speed, ACROSS)])
    left = after(left, speed)
    parts = []
    for near in range(SIDE):
        total = base[near] - mine[near]
        for piece in (far, right, left):
            total = total + (base[near] - piece[near])
        parts.append(total)
    got = [send(parts[step], SECOND[step]) for step in (2, 1, 3)]
    pair = parts[0] + got[0] + got[1] + got[2]

    other = send(pair, ACROSS)
    summed = pair + jnp.stack([other[1], other[0]])
    speeds = spread_near(after(speed, pair))
    summed = after(summed, *speeds)
    average = summed / islands
    nears = spread_near(average)

    count = rows * columns * shards
    squares = jnp.broadcast_to(jnp.sum(average * average).reshape(1, 1), (8, 128))
    squares = squares + send(squares, TWIN)
    for route in (UP, SECOND, FIRST):
        squares = squares + send(squares, route[1]) + send(squares, route[2]) + send(squares, route[3])
    spread = jnp.sqrt(squares[0, 0] / count + 1e-06)
    factor = jnp.minimum(1.0, clip_level / spread)

    def update(base, average, speed):
        clipped = factor * average
        return base - outer_rate * (clipped + moment_decay * (moment_decay * speed + clipped))

    new_momentum = moment_decay * momentum + factor * average[0]
    early = jnp.stack([update(base[k], nears[k], speeds[k]) for k in range(2)])
    late = jnp.stack([update(base[2 + k], nears[2 + k], speeds[2 + k]) for k in range(2)])

    left_early, right_late = send(early, FIRST[1]), send(late, FIRST[3])
    left_late, right_early = send(late, FIRST[1]), send(early, FIRST[3])
    far_early, far_late = send(left_early, FIRST[1]), send(right_late, FIRST[3])
    groups = ((0, 0), (0, 1), (3, 0), (1, 1), (3, 1), (1, 0), (2, 0), (2, 1))
    pieces = (early, late, left_early, right_late, left_late, right_early, far_early, far_late)
    new_global = None
    for n in range(0, len(groups), 2):
        new_global = unpack(groups[n : n + 2], pieces[n : n + 2], new_global, (rows, columns))
    return (new_global, new_momentum)


def solution(mesh):
    placed = (P("fsdp", None), P("island", "fsdp", None), P("fsdp", "island"))
    return jax.shard_map(
        per_device,
        mesh=mesh,
        in_specs=placed,
        out_specs=(P("fsdp", None), P("fsdp", "island")),
        check_vma=False,
    )
```

```python
import functools

import jax
import jax.numpy as jnp
from jax import lax
from jax.experimental import pallas as pl
from jax.experimental.pallas import tpu as pltpu
from jax.sharding import PartitionSpec as P

clip_level = 0.1
outer_rate = 0.7
moment_decay = 0.9

AXES = ("island", "fsdp")
HALVES, SIDE, RUN, CORES = 2, 4, 4, 2
BLOCKS = 2 * HALVES
ROOM = 16 * 2**20


def pairs(move):
    out = []
    for zh in range(HALVES):
        for x in range(SIDE):
            for y in range(SIDE):
                for zl in range(RUN):
                    for core in range(CORES):
                        there = move(zh, x, y, zl, core)
                        place = lambda h, i, j, k, c: ((h * SIDE + i) * SIDE + j) * RUN * CORES + k * CORES + c
                        out.append((place(zh, x, y, zl, core), place(*there)))
    return out


def along(first, step):
    def move(zh, x, y, zl, core):
        if (core == 0) == first:
            return zh, (x + step) % SIDE, y, zl, core
        return zh, x, (y + step) % SIDE, zl, core

    return pairs(move)


FIRST = {step: along(True, step) for step in (1, 2, 3)}
SECOND = {step: along(False, step) for step in (1, 2, 3)}
ACROSS = pairs(lambda zh, x, y, zl, core: (1 - zh, x, y, zl, core))
UP = {step: pairs(lambda zh, x, y, zl, core, s=step: (zh, x, y, (zl + s) % RUN, core)) for step in (1, 2, 3)}
TWIN = pairs(lambda zh, x, y, zl, core: (zh, x, y, zl, 1 - core))


def send(value, route):
    return lax.ppermute(value, AXES, route)


def place_of(width, step, near, half):
    island = lax.axis_index("island")
    core = lax.rem(lax.axis_index("fsdp"), CORES)
    zh = island // (SIDE * SIDE)
    x = lax.rem(island // SIDE, SIDE)
    y = lax.rem(island, SIDE)
    one = jnp.where(core == 0, x, y)
    two = jnp.where(core == 0, y, x)
    one = lax.rem(one + step, SIDE)
    two = lax.rem(two + near, SIDE)
    zh = lax.rem(zh + half, HALVES)
    block = zh * SIDE * SIDE + jnp.where(core == 0, one * SIDE + two, two * SIDE + one)
    return pl.multiple_of(block * width, 128)


def blocks_of(groups):
    return [(step, 2 * group + k, half) for step, group in groups for k in range(2) for half in range(HALVES)]


def pack_kernel(jobs, width, *refs):
    sems = refs[-1]
    inputs = len(refs) - 1 - len(jobs)
    copies = []
    for n, (source, step) in enumerate(jobs):
        for near in range(SIDE):
            for half in range(HALVES):
                copy = pltpu.make_async_copy(
                    refs[source].at[:, pl.ds(place_of(width, step, near, half), width)],
                    refs[inputs + n].at[near, half],
                    sems.at[len(copies)],
                )
                copy.start()
                copies.append(copy)
    for copy in copies:
        copy.wait()


def pack(sources, jobs, width, behind=()):
    rows = sources[0].shape[0]
    amount = len(jobs) * SIDE * HALVES
    return pl.pallas_call(
        functools.partial(pack_kernel, jobs, width),
        out_shape=[jax.ShapeDtypeStruct((SIDE, HALVES, rows, width), sources[0].dtype)] * len(jobs),
        in_specs=[pl.BlockSpec(memory_space=pltpu.HBM)] * len(sources)
        + [pl.BlockSpec(memory_space=pl.ANY)] * len(behind),
        out_specs=[pl.BlockSpec(memory_space=pltpu.VMEM)] * len(jobs),
        scratch_shapes=[pltpu.SemaphoreType.DMA((amount,))],
        cost_estimate=pl.CostEstimate(flops=0, bytes_accessed=8 * amount * rows * width, transcendentals=0),
        compiler_params=pltpu.CompilerParams(vmem_limit_bytes=ROOM),
        name=f"pack{len(jobs)}",
    )(*sources, *behind)


def unpack_kernel(groups, width, *refs):
    pieces, (whole, sems) = refs[: len(groups)], refs[-2:]
    copies = []
    for n, block in enumerate(blocks_of(groups)):
        group, k, half = n // BLOCKS, (n % BLOCKS) // HALVES, n % HALVES
        copy = pltpu.make_async_copy(
            pieces[group].at[k, half], whole.at[:, pl.ds(place_of(width, *block), width)], sems.at[n]
        )
        copy.start()
        copies.append(copy)
    for copy in copies:
        copy.wait()


def unpack(groups, pieces, whole, shape):
    rows, width = pieces[0].shape[-2:]
    given = [] if whole is None else [whole]
    vmem, hbm = pl.BlockSpec(memory_space=pltpu.VMEM), pl.BlockSpec(memory_space=pltpu.HBM)
    amount = len(groups) * BLOCKS
    return pl.pallas_call(
        functools.partial(unpack_kernel, groups, width),
        out_shape=jax.ShapeDtypeStruct(shape, pieces[0].dtype),
        in_specs=[vmem] * len(groups) + [hbm] * len(given),
        out_specs=hbm,
        scratch_shapes=[pltpu.SemaphoreType.DMA((amount,))],
        input_output_aliases={len(groups): 0} if given else {},
        cost_estimate=pl.CostEstimate(flops=0, bytes_accessed=8 * amount * rows * width, transcendentals=0),
        compiler_params=pltpu.CompilerParams(vmem_limit_bytes=ROOM),
        name=f"unpack{len(groups)}",
    )(*pieces, *given)


def squares_kernel(value, total):
    halves, rows, width = value.shape
    sums = jnp.zeros((8, 128), jnp.float32)
    for half in range(halves):
        for row in range(0, rows, 8):
            for column in range(0, width, 128):
                tile = value[half, row : row + 8, column : column + 128]
                sums = sums + tile * tile
    total[...] = sums


def squares_of(value):
    return pl.pallas_call(
        squares_kernel,
        out_shape=jax.ShapeDtypeStruct((8, 128), value.dtype),
        in_specs=[pl.BlockSpec(memory_space=pltpu.VMEM)],
        out_specs=pl.BlockSpec(memory_space=pltpu.VMEM),
        cost_estimate=pl.CostEstimate(flops=2 * value.size, bytes_accessed=4 * value.size, transcendentals=0),
        compiler_params=pltpu.CompilerParams(vmem_limit_bytes=ROOM),
        name="squares",
    )(value)


def update_kernel(count, *refs):
    squares, base, averages, speeds = refs[:SIDE], refs[SIDE], refs[SIDE + 1 : 2 * SIDE + 1], refs[2 * SIDE + 1 : -3]
    early, late, kept = refs[-3:]
    total = squares[0][...]
    for more in squares[1:]:
        total = total + more[...]
    total = jnp.sum(jnp.sum(total, axis=0, keepdims=True), axis=1, keepdims=True)
    factor = jnp.minimum(1.0, clip_level / jnp.sqrt(total / count + 1e-06))
    for near in range(SIDE):
        for half in range(HALVES):
            clipped = factor * averages[near][half]
            new_momentum = moment_decay * speeds[near][half] + clipped
            if near == half == 0:
                kept[...] = new_momentum
            (early if near < 2 else late)[near % 2, half] = base[near, half] - outer_rate * (
                clipped + moment_decay * new_momentum
            )


def update(squares, base, averages, speeds, count):
    rows, width = base.shape[-2:]
    part = jax.ShapeDtypeStruct((2, HALVES, rows, width), base.dtype)
    vmem = pl.BlockSpec(memory_space=pltpu.VMEM)
    return pl.pallas_call(
        functools.partial(update_kernel, count),
        out_shape=[part, part, jax.ShapeDtypeStruct((rows, width), base.dtype)],
        in_specs=[vmem] * (1 + 3 * SIDE),
        out_specs=[vmem] * 3,
        cost_estimate=pl.CostEstimate(flops=8 * base.size, bytes_accessed=16 * base.size, transcendentals=0),
        compiler_params=pltpu.CompilerParams(vmem_limit_bytes=ROOM),
        name="update",
    )(*squares, base, *averages, *speeds)


def spread_near(value):
    near = [value] + [None] * (SIDE - 1)
    for step in (2, 1, 3):
        near[SIDE - step] = send(value, SECOND[step])
    return near


def exchange(value, route):
    return value + send(value, route[1]) + send(value, route[2]) + send(value, route[3])


def after(value, *others):
    return lax.optimization_barrier((value,) + others)[0]


def per_device(global_weights, local_weights, momentum):
    islands = lax.axis_size("island")
    shards = lax.axis_size("fsdp")
    rows, columns = global_weights.shape
    width = columns // islands
    local = local_weights[0]

    (far,) = pack((local,), ((0, 2),), width)
    right, left = pack((local,), ((0, 1), (0, 3)), width, (far,))
    up, down = send(far[:2], FIRST[1]), send(far[2:], FIRST[3])
    from_left, from_right = send(right[2:], FIRST[1]), send(left[:2], FIRST[3])
    base, base_right, base_left, mine = pack(
        (global_weights, local), ((0, 0), (0, 1), (0, 3), (1, 0)), width, (left,)
    )
    up = (base_right[:2] - right[:2]) + (base_right[:2] - up)
    down = (base_left[2:] - left[2:]) + (base_left[2:] - down)
    speed = after(momentum, base)
    speed = jnp.stack([speed, send(speed, ACROSS)])
    relay_up, relay_down = send(up, FIRST[1]), send(down, FIRST[3])
    relay_up = after(relay_up, speed)
    parts = []
    for near in range(SIDE):
        k = near % 2
        total = base[near] - mine[near]
        if near < 2:
            total = total + (base[near] - from_right[k]) + relay_up[k]
        else:
            total = total + (base[near] - from_left[k]) + relay_down[k]
        parts.append(total)
    got = [send(parts[step], SECOND[step]) for step in (2, 1, 3)]
    pair = parts[0] + got[0] + got[1] + got[2]

    other = send(pair, ACROSS)
    summed = pair + jnp.stack([other[1], other[0]])
    speeds = spread_near(after(speed, pair))
    average = summed / islands
    nears = spread_near(average)

    count = rows * columns * shards
    squares = squares_of(average)
    squares = squares + send(squares, TWIN)
    squares = after(squares, *speeds)
    squares = exchange(squares, UP)
    squares = exchange(squares, SECOND)
    squares = [squares] + [send(squares, FIRST[step]) for step in (1, 2, 3)]
    early, late, new_momentum = update(squares, base, nears, speeds, count)

    left_early, right_late = send(early, FIRST[1]), send(late, FIRST[3])
    left_late, right_early = send(late, FIRST[1]), send(early, FIRST[3])
    far_early, far_late = send(left_early, FIRST[1]), send(right_late, FIRST[3])
    groups = ((0, 0), (0, 1), (3, 0), (1, 1), (3, 1), (1, 0), (2, 0), (2, 1))
    pieces = (early, late, left_early, right_late, left_late, right_early, far_early, far_late)
    new_global = None
    for n in range(0, len(groups), 2):
        new_global = unpack(groups[n : n + 2], pieces[n : n + 2], new_global, (rows, columns))
    return (new_global, new_momentum)


def solution(mesh):
    placed = (P("fsdp", None), P("island", "fsdp", None), P("fsdp", "island"))
    return jax.shard_map(
        per_device,
        mesh=mesh,
        in_specs=placed,
        out_specs=(P("fsdp", None), P("fsdp", "island")),
        check_vma=False,
    )
```

```python
import functools

import jax
import jax.numpy as jnp
from jax import lax
from jax.experimental import pallas as pl
from jax.experimental.pallas import tpu as pltpu
from jax.sharding import PartitionSpec as P

clip_level = 0.1
outer_rate = 0.7
moment_decay = 0.9

AXES = ("island", "fsdp")
HALVES, SIDE, RUN, CORES = 2, 4, 4, 2
BLOCKS = 2 * HALVES
ROOM = 16 * 2**20


def pairs(move):
    out = []
    for zh in range(HALVES):
        for x in range(SIDE):
            for y in range(SIDE):
                for zl in range(RUN):
                    for core in range(CORES):
                        there = move(zh, x, y, zl, core)
                        place = lambda h, i, j, k, c: ((h * SIDE + i) * SIDE + j) * RUN * CORES + k * CORES + c
                        out.append((place(zh, x, y, zl, core), place(*there)))
    return out


def along(first, step):
    def move(zh, x, y, zl, core):
        if (core == 0) == first:
            return zh, (x + step) % SIDE, y, zl, core
        return zh, x, (y + step) % SIDE, zl, core

    return pairs(move)


FIRST = {step: along(True, step) for step in (1, 2, 3)}
SECOND = {step: along(False, step) for step in (1, 2, 3)}
ACROSS = pairs(lambda zh, x, y, zl, core: (1 - zh, x, y, zl, core))
UP = {step: pairs(lambda zh, x, y, zl, core, s=step: (zh, x, y, (zl + s) % RUN, core)) for step in (1, 2, 3)}
TWIN = pairs(lambda zh, x, y, zl, core: (zh, x, y, zl, 1 - core))


def send(value, route):
    return lax.ppermute(value, AXES, route)


def place_of(width, step, near, half):
    island = lax.axis_index("island")
    core = lax.rem(lax.axis_index("fsdp"), CORES)
    zh = island // (SIDE * SIDE)
    x = lax.rem(island // SIDE, SIDE)
    y = lax.rem(island, SIDE)
    one = jnp.where(core == 0, x, y)
    two = jnp.where(core == 0, y, x)
    one = lax.rem(one + step, SIDE)
    two = lax.rem(two + near, SIDE)
    zh = lax.rem(zh + half, HALVES)
    block = zh * SIDE * SIDE + jnp.where(core == 0, one * SIDE + two, two * SIDE + one)
    return pl.multiple_of(block * width, 128)


def blocks_of(groups):
    return [(step, 2 * group + k, half) for step, group in groups for k in range(2) for half in range(HALVES)]


def pack_kernel(jobs, width, *refs):
    sems = refs[-1]
    inputs = len(refs) - 1 - len(jobs)
    copies = []
    for n, (source, step) in enumerate(jobs):
        for near in range(SIDE):
            for half in range(HALVES):
                copy = pltpu.make_async_copy(
                    refs[source].at[:, pl.ds(place_of(width, step, near, half), width)],
                    refs[inputs + n].at[near, half],
                    sems.at[len(copies)],
                )
                copy.start()
                copies.append(copy)
    for copy in copies:
        copy.wait()


def pack(sources, jobs, width, behind=()):
    rows = sources[0].shape[0]
    amount = len(jobs) * SIDE * HALVES
    return pl.pallas_call(
        functools.partial(pack_kernel, jobs, width),
        out_shape=[jax.ShapeDtypeStruct((SIDE, HALVES, rows, width), sources[0].dtype)] * len(jobs),
        in_specs=[pl.BlockSpec(memory_space=pltpu.HBM)] * len(sources)
        + [pl.BlockSpec(memory_space=pl.ANY)] * len(behind),
        out_specs=[pl.BlockSpec(memory_space=pltpu.VMEM)] * len(jobs),
        scratch_shapes=[pltpu.SemaphoreType.DMA((amount,))],
        cost_estimate=pl.CostEstimate(flops=0, bytes_accessed=8 * amount * rows * width, transcendentals=0),
        compiler_params=pltpu.CompilerParams(vmem_limit_bytes=ROOM),
        name=f"pack{len(jobs)}",
    )(*sources, *behind)


def unpack_kernel(groups, width, *refs):
    pieces, (whole, sems) = refs[: len(groups)], refs[-2:]
    copies = []
    for n, block in enumerate(blocks_of(groups)):
        group, k, half = n // BLOCKS, (n % BLOCKS) // HALVES, n % HALVES
        copy = pltpu.make_async_copy(
            pieces[group].at[k, half], whole.at[:, pl.ds(place_of(width, *block), width)], sems.at[n]
        )
        copy.start()
        copies.append(copy)
    for copy in copies:
        copy.wait()


def unpack(groups, pieces, whole, shape):
    rows, width = pieces[0].shape[-2:]
    given = [] if whole is None else [whole]
    vmem, hbm = pl.BlockSpec(memory_space=pltpu.VMEM), pl.BlockSpec(memory_space=pltpu.HBM)
    amount = len(groups) * BLOCKS
    return pl.pallas_call(
        functools.partial(unpack_kernel, groups, width),
        out_shape=jax.ShapeDtypeStruct(shape, pieces[0].dtype),
        in_specs=[vmem] * len(groups) + [hbm] * len(given),
        out_specs=hbm,
        scratch_shapes=[pltpu.SemaphoreType.DMA((amount,))],
        input_output_aliases={len(groups): 0} if given else {},
        cost_estimate=pl.CostEstimate(flops=0, bytes_accessed=8 * amount * rows * width, transcendentals=0),
        compiler_params=pltpu.CompilerParams(vmem_limit_bytes=ROOM),
        name=f"unpack{len(groups)}",
    )(*pieces, *given)


def squares_kernel(value, total):
    halves, rows, width = value.shape
    sums = jnp.zeros((8, 128), jnp.float32)
    for half in range(halves):
        for row in range(0, rows, 8):
            for column in range(0, width, 128):
                tile = value[half, row : row + 8, column : column + 128]
                sums = sums + tile * tile
    total[...] = sums


def squares_of(value):
    return pl.pallas_call(
        squares_kernel,
        out_shape=jax.ShapeDtypeStruct((8, 128), value.dtype),
        in_specs=[pl.BlockSpec(memory_space=pltpu.VMEM)],
        out_specs=pl.BlockSpec(memory_space=pltpu.VMEM),
        cost_estimate=pl.CostEstimate(flops=2 * value.size, bytes_accessed=4 * value.size, transcendentals=0),
        compiler_params=pltpu.CompilerParams(vmem_limit_bytes=ROOM),
        name="squares",
    )(value)


def update_kernel(count, *refs):
    squares, base, averages, speeds = refs[:SIDE], refs[SIDE], refs[SIDE + 1 : 2 * SIDE + 1], refs[2 * SIDE + 1 : -3]
    early, late, kept = refs[-3:]
    total = squares[0][...]
    for more in squares[1:]:
        total = total + more[...]
    total = jnp.sum(jnp.sum(total, axis=0, keepdims=True), axis=1, keepdims=True)
    factor = jnp.minimum(1.0, clip_level / jnp.sqrt(total / count + 1e-06))
    for near in range(SIDE):
        for half in range(HALVES):
            clipped = factor * averages[near][half]
            new_momentum = moment_decay * speeds[near][half] + clipped
            if near == half == 0:
                kept[...] = new_momentum
            (early if near < 2 else late)[near % 2, half] = base[near, half] - outer_rate * (
                clipped + moment_decay * new_momentum
            )


def update(squares, base, averages, speeds, count):
    rows, width = base.shape[-2:]
    part = jax.ShapeDtypeStruct((2, HALVES, rows, width), base.dtype)
    vmem = pl.BlockSpec(memory_space=pltpu.VMEM)
    return pl.pallas_call(
        functools.partial(update_kernel, count),
        out_shape=[part, part, jax.ShapeDtypeStruct((rows, width), base.dtype)],
        in_specs=[vmem] * (1 + 3 * SIDE),
        out_specs=[vmem] * 3,
        cost_estimate=pl.CostEstimate(flops=8 * base.size, bytes_accessed=16 * base.size, transcendentals=0),
        compiler_params=pltpu.CompilerParams(vmem_limit_bytes=ROOM),
        name="update",
    )(*squares, base, *averages, *speeds)


def spread_near(value):
    near = [value] + [None] * (SIDE - 1)
    for step in (2, 1, 3):
        near[SIDE - step] = send(value, SECOND[step])
    return near


def exchange(value, route):
    return value + send(value, route[1]) + send(value, route[2]) + send(value, route[3])


def after(value, *others):
    return lax.optimization_barrier((value,) + others)[0]


def per_device(global_weights, local_weights, momentum):
    islands = lax.axis_size("island")
    shards = lax.axis_size("fsdp")
    rows, columns = global_weights.shape
    width = columns // islands
    local = pltpu.with_memory_space_constraint(local_weights[0], pltpu.HBM)

    (far,) = pack((local,), ((0, 2),), width)
    right, left = pack((local,), ((0, 1), (0, 3)), width, (far,))
    up, down = send(far[:2], FIRST[1]), send(far[2:], FIRST[3])
    from_left, from_right = send(right[2:], FIRST[1]), send(left[:2], FIRST[3])
    base, base_right, base_left, mine = pack(
        (global_weights, local), ((0, 0), (0, 1), (0, 3), (1, 0)), width, (left,)
    )
    up = (base_right[:2] - right[:2]) + (base_right[:2] - up)
    down = (base_left[2:] - left[2:]) + (base_left[2:] - down)
    speed = after(momentum, base)
    speed = jnp.stack([speed, send(speed, ACROSS)])
    relay_up, relay_down = send(up, FIRST[1]), send(down, FIRST[3])
    relay_up = after(relay_up, speed)
    parts = []
    for near in range(SIDE):
        k = near % 2
        total = base[near] - mine[near]
        if near < 2:
            total = total + (base[near] - from_right[k]) + relay_up[k]
        else:
            total = total + (base[near] - from_left[k]) + relay_down[k]
        parts.append(total)
    got = [send(parts[step], SECOND[step]) for step in (2, 1, 3)]
    pair = parts[0] + got[0] + got[1] + got[2]

    other = send(pair, ACROSS)
    summed = pair + jnp.stack([other[1], other[0]])
    speeds = spread_near(after(speed, pair))
    average = summed / islands
    nears = spread_near(average)

    count = rows * columns * shards
    squares = squares_of(average)
    squares = squares + send(squares, TWIN)
    squares = after(squares, *speeds)
    squares = exchange(squares, UP)
    squares = exchange(squares, SECOND)
    squares = [squares] + [send(squares, FIRST[step]) for step in (1, 2, 3)]
    early, late, new_momentum = update(squares, base, nears, speeds, count)

    left_early, right_late = send(early, FIRST[1]), send(late, FIRST[3])
    left_late, right_early = send(late, FIRST[1]), send(early, FIRST[3])
    far_early, far_late = send(left_early, FIRST[1]), send(right_late, FIRST[3])
    groups = ((0, 0), (0, 1), (3, 0), (1, 1), (3, 1), (1, 0), (2, 0), (2, 1))
    pieces = (early, late, left_early, right_late, left_late, right_early, far_early, far_late)
    new_global = None
    for n in range(0, len(groups), 2):
        new_global = unpack(groups[n : n + 2], pieces[n : n + 2], new_global, (rows, columns))
    return (new_global, new_momentum)


def solution(mesh):
    placed = (P("fsdp", None), P("island", "fsdp", None), P("fsdp", "island"))
    return jax.shard_map(
        per_device,
        mesh=mesh,
        in_specs=placed,
        out_specs=(P("fsdp", None), P("fsdp", "island")),
        check_vma=False,
    )
```

```python
import functools

import jax
import jax.numpy as jnp
from jax import lax
from jax.experimental import pallas as pl
from jax.experimental.pallas import tpu as pltpu
from jax.sharding import PartitionSpec as P

clip_level = 0.1
outer_rate = 0.7
moment_decay = 0.9

AXES = ("island", "fsdp")
HALVES, SIDE, RUN, CORES = 2, 4, 4, 2
BLOCKS = 2 * HALVES
ROOM = 16 * 2**20


def pairs(move):
    out = []
    for zh in range(HALVES):
        for x in range(SIDE):
            for y in range(SIDE):
                for zl in range(RUN):
                    for core in range(CORES):
                        there = move(zh, x, y, zl, core)
                        place = lambda h, i, j, k, c: ((h * SIDE + i) * SIDE + j) * RUN * CORES + k * CORES + c
                        out.append((place(zh, x, y, zl, core), place(*there)))
    return out


def along(first, step):
    def move(zh, x, y, zl, core):
        if (core == 0) == first:
            return zh, (x + step) % SIDE, y, zl, core
        return zh, x, (y + step) % SIDE, zl, core

    return pairs(move)


FIRST = {step: along(True, step) for step in (1, 2, 3)}
SECOND = {step: along(False, step) for step in (1, 2, 3)}
ACROSS = pairs(lambda zh, x, y, zl, core: (1 - zh, x, y, zl, core))
UP = {step: pairs(lambda zh, x, y, zl, core, s=step: (zh, x, y, (zl + s) % RUN, core)) for step in (1, 2, 3)}
TWIN = pairs(lambda zh, x, y, zl, core: (zh, x, y, zl, 1 - core))


def send(value, route):
    return lax.ppermute(value, AXES, route)


def place_of(width, step, near, half):
    island = lax.axis_index("island")
    core = lax.rem(lax.axis_index("fsdp"), CORES)
    zh = island // (SIDE * SIDE)
    x = lax.rem(island // SIDE, SIDE)
    y = lax.rem(island, SIDE)
    one = jnp.where(core == 0, x, y)
    two = jnp.where(core == 0, y, x)
    one = lax.rem(one + step, SIDE)
    two = lax.rem(two + near, SIDE)
    zh = lax.rem(zh + half, HALVES)
    block = zh * SIDE * SIDE + jnp.where(core == 0, one * SIDE + two, two * SIDE + one)
    return pl.multiple_of(block * width, 128)


def blocks_of(groups):
    return [(step, 2 * group + k, half) for step, group in groups for k in range(2) for half in range(HALVES)]


def pack_kernel(jobs, width, *refs):
    sems = refs[-1]
    inputs = len(refs) - 1 - len(jobs)
    copies = []
    for n, (source, step) in enumerate(jobs):
        for near in range(SIDE):
            for half in range(HALVES):
                copy = pltpu.make_async_copy(
                    refs[source].at[:, pl.ds(place_of(width, step, near, half), width)],
                    refs[inputs + n].at[near, half],
                    sems.at[len(copies)],
                )
                copy.start()
                copies.append(copy)
    for copy in copies:
        copy.wait()


def pack(sources, jobs, width, behind=()):
    rows = sources[0].shape[0]
    amount = len(jobs) * SIDE * HALVES
    return pl.pallas_call(
        functools.partial(pack_kernel, jobs, width),
        out_shape=[jax.ShapeDtypeStruct((SIDE, HALVES, rows, width), sources[0].dtype)] * len(jobs),
        in_specs=[pl.BlockSpec(memory_space=pltpu.HBM)] * len(sources)
        + [pl.BlockSpec(memory_space=pl.ANY)] * len(behind),
        out_specs=[pl.BlockSpec(memory_space=pltpu.VMEM)] * len(jobs),
        scratch_shapes=[pltpu.SemaphoreType.DMA((amount,))],
        cost_estimate=pl.CostEstimate(flops=0, bytes_accessed=8 * amount * rows * width, transcendentals=0),
        compiler_params=pltpu.CompilerParams(vmem_limit_bytes=ROOM),
        name=f"pack{len(jobs)}",
    )(*sources, *behind)


def unpack_kernel(groups, width, *refs):
    pieces, (whole, sems) = refs[: len(groups)], refs[-2:]
    copies = []
    for n, block in enumerate(blocks_of(groups)):
        group, k, half = n // BLOCKS, (n % BLOCKS) // HALVES, n % HALVES
        copy = pltpu.make_async_copy(
            pieces[group].at[k, half], whole.at[:, pl.ds(place_of(width, *block), width)], sems.at[n]
        )
        copy.start()
        copies.append(copy)
    for copy in copies:
        copy.wait()


def unpack(groups, pieces, whole, shape):
    rows, width = pieces[0].shape[-2:]
    given = [] if whole is None else [whole]
    vmem, hbm = pl.BlockSpec(memory_space=pltpu.VMEM), pl.BlockSpec(memory_space=pltpu.HBM)
    amount = len(groups) * BLOCKS
    return pl.pallas_call(
        functools.partial(unpack_kernel, groups, width),
        out_shape=jax.ShapeDtypeStruct(shape, pieces[0].dtype),
        in_specs=[vmem] * len(groups) + [hbm] * len(given),
        out_specs=hbm,
        scratch_shapes=[pltpu.SemaphoreType.DMA((amount,))],
        input_output_aliases={len(groups): 0} if given else {},
        cost_estimate=pl.CostEstimate(flops=0, bytes_accessed=8 * amount * rows * width, transcendentals=0),
        compiler_params=pltpu.CompilerParams(vmem_limit_bytes=ROOM),
        name=f"unpack{len(groups)}",
    )(*pieces, *given)


def squares_kernel(value, total):
    halves, rows, width = value.shape
    sums = jnp.zeros((8, 128), jnp.float32)
    for half in range(halves):
        for row in range(0, rows, 8):
            for column in range(0, width, 128):
                tile = value[half, row : row + 8, column : column + 128]
                sums = sums + tile * tile
    total[...] = sums


def squares_of(value):
    return pl.pallas_call(
        squares_kernel,
        out_shape=jax.ShapeDtypeStruct((8, 128), value.dtype),
        in_specs=[pl.BlockSpec(memory_space=pltpu.VMEM)],
        out_specs=pl.BlockSpec(memory_space=pltpu.VMEM),
        cost_estimate=pl.CostEstimate(flops=2 * value.size, bytes_accessed=4 * value.size, transcendentals=0),
        compiler_params=pltpu.CompilerParams(vmem_limit_bytes=ROOM),
        name="squares",
    )(value)


def update_kernel(count, *refs):
    squares, base, averages, speeds = refs[:SIDE], refs[SIDE], refs[SIDE + 1 : 2 * SIDE + 1], refs[2 * SIDE + 1 : -3]
    early, late, kept = refs[-3:]
    total = squares[0][...]
    for more in squares[1:]:
        total = total + more[...]
    total = jnp.sum(jnp.sum(total, axis=0, keepdims=True), axis=1, keepdims=True)
    factor = jnp.minimum(1.0, clip_level / jnp.sqrt(total / count + 1e-06))
    for near in range(SIDE):
        for half in range(HALVES):
            clipped = factor * averages[near][half]
            new_momentum = moment_decay * speeds[near][half] + clipped
            if near == half == 0:
                kept[...] = new_momentum
            (early if near < 2 else late)[near % 2, half] = base[near, half] - outer_rate * (
                clipped + moment_decay * new_momentum
            )


def update(squares, base, averages, speeds, count):
    rows, width = base.shape[-2:]
    part = jax.ShapeDtypeStruct((2, HALVES, rows, width), base.dtype)
    vmem = pl.BlockSpec(memory_space=pltpu.VMEM)
    return pl.pallas_call(
        functools.partial(update_kernel, count),
        out_shape=[part, part, jax.ShapeDtypeStruct((rows, width), base.dtype)],
        in_specs=[vmem] * (1 + 3 * SIDE),
        out_specs=[vmem] * 3,
        cost_estimate=pl.CostEstimate(flops=8 * base.size, bytes_accessed=16 * base.size, transcendentals=0),
        compiler_params=pltpu.CompilerParams(vmem_limit_bytes=ROOM),
        name="update",
    )(*squares, base, *averages, *speeds)


def spread_near(value):
    near = [value] + [None] * (SIDE - 1)
    for step in (2, 1, 3):
        near[SIDE - step] = send(value, SECOND[step])
    return near


def exchange(value, route):
    return value + send(value, route[1]) + send(value, route[2]) + send(value, route[3])


def after(value, *others):
    return lax.optimization_barrier((value,) + others)[0]


def per_device(global_weights, local_weights, momentum):
    islands = lax.axis_size("island")
    shards = lax.axis_size("fsdp")
    rows, columns = global_weights.shape
    width = columns // islands
    local = pltpu.with_memory_space_constraint(local_weights[0], pltpu.HBM)

    (far,) = pack((local,), ((0, 2),), width)
    right, left = pack((local,), ((0, 1), (0, 3)), width, (far,))
    up, down = send(far[:2], FIRST[1]), send(far[2:], FIRST[3])
    from_left, from_right = send(right[2:], FIRST[1]), send(left[:2], FIRST[3])
    base, base_right, base_left, mine = pack(
        (global_weights, local), ((0, 0), (0, 1), (0, 3), (1, 0)), width, (left,)
    )
    up = (base_right[:2] - right[:2]) + (base_right[:2] - up)
    down = (base_left[2:] - left[2:]) + (base_left[2:] - down)
    speed = after(momentum, base)
    speed = jnp.stack([speed, send(speed, ACROSS)])
    relay_up, relay_down = send(up, FIRST[1]), send(down, FIRST[3])
    relay_up = after(relay_up, speed)
    parts = []
    for near in range(SIDE):
        k = near % 2
        total = base[near] - mine[near]
        if near < 2:
            total = total + (base[near] - from_right[k]) + relay_up[k]
        else:
            total = total + (base[near] - from_left[k]) + relay_down[k]
        parts.append(total)
    got = [send(parts[step], SECOND[step]) for step in (2, 1, 3)]
    pair = parts[0] + got[0] + got[1] + got[2]

    other = send(pair, ACROSS)
    summed = pair + jnp.stack([other[1], other[0]])
    speeds = spread_near(after(speed, pair))
    average = summed / islands
    nears = spread_near(average)

    count = rows * columns * shards
    squares = squares_of(average)
    squares = squares + send(squares, TWIN)
    squares = after(squares, *speeds)
    squares = exchange(squares, UP)
    squares = exchange(squares, SECOND)
    squares = [squares] + [send(squares, FIRST[step]) for step in (1, 2, 3)]
    early, late, new_momentum = update(squares, base, nears, speeds, count)

    left_early, right_late = send(early, FIRST[1]), send(late, FIRST[3])
    left_late, right_early = send(late, FIRST[1]), send(early, FIRST[3])
    far_early, far_late = send(left_early, FIRST[1]), send(right_late, FIRST[3])
    groups = ((0, 0), (0, 1), (3, 0), (1, 1), (3, 1), (1, 0), (2, 0), (2, 1))
    pieces = (early, late, left_early, right_late, left_late, right_early, far_early, far_late)
    new_global = unpack(groups[:4], pieces[:4], None, (rows, columns))
    for n in (4, 6):
        new_global = unpack(groups[n : n + 2], pieces[n : n + 2], new_global, (rows, columns))
    return (new_global, new_momentum)


def solution(mesh):
    placed = (P("fsdp", None), P("island", "fsdp", None), P("fsdp", "island"))
    return jax.shard_map(
        per_device,
        mesh=mesh,
        in_specs=placed,
        out_specs=(P("fsdp", None), P("fsdp", "island")),
        check_vma=False,
    )
```
